128 devices in a mesh: dp: 16 (over y, x), mp: 8 (over z, core).
Axes of the slice: x: 4, y: 4, z: 4, core: 2. Of those that a mesh axis runs over, the one named last changes fastest.
Arguments:
- train_in: bfloat16 [128, 256, 11008], P('dp', None, 'mp'), may hold values from -6 to 6
- train_grad_out: bfloat16 [128, 256, 4096], P('dp', None, 'mp'), as said below
- target_in: bfloat16 [128, 256, 11008], P('dp', None, 'mp'), may hold values from -6 to 6
- target_grad_out: bfloat16 [128, 256, 4096], P('dp', None, 'mp'), as said below
- proj_in: bfloat16 [64, 11008], P(None, 'mp'), may hold values from -0.0546875 to 0.0546875
- proj_out: bfloat16 [64, 4096], P(None, 'mp'), may hold values from -0.09375 to 0.09375
Outputs:
- scores: float32 [128, 128], P(('dp', 'mp'))
The draws below stay inside these ranges and needn't reach their ends.
Inputs may be any that keep to these rules, and one draw needn't show every extreme that they name: `train_grad_out`: every example's output gradients share one positive scale, different from example to example. `target_grad_out`: every example's output gradients share one positive scale, different from example to example.
All inputs are finite; a program needn't handle non-finite values.
Results may differ from the reference program's by a relative error of at most 0.00055.
Values sent between devices are 32-bit elements; how exact they have to be, the bound alone decides.
A program may use at most 128 MiB of HBM per device.

```python
import math
import jax
import jax.numpy as jnp
from jax import lax

DIN = 11008
DOUT = 4096
RANK = 64
SEQ = 256
ITERS = 4
NTRAIN = 128
NTGT = 128


def scaled_grads(key, count):
    key_scale, key_base = jax.random.split(key)
    ramp = 1.0 + 2.0 * jnp.arange(count, dtype=jnp.float32) / max(count - 1, 1)
    scales = jnp.exp(jax.random.uniform(key_scale, (count,), jnp.float32, 0.0, math.log(10.0))) * ramp
    base = jnp.clip(jax.random.normal(key_base, (count, SEQ, DOUT), jnp.float32), -6.0, 6.0)
    return (base * scales[:, None, None]).astype(jnp.bfloat16)


def draw_train_grad_out(key, part):
    key = jax.random.fold_in(key, 11)
    return scaled_grads(key, NTRAIN)


def draw_target_grad_out(key, part):
    key = jax.random.fold_in(key, 23)
    return scaled_grads(key, NTGT)


def levels(key, shape, pieces, smallest, top_value):
    factor_of, own = 1.0, jax.random.fold_in(key, 6)
    for dim, blocks in pieces:
        steps = jnp.exp(jax.random.uniform(jax.random.fold_in(own, dim), (blocks,), jnp.float32, smallest / len(pieces), top_value / len(pieces)))
        factor_of = factor_of * jnp.repeat(steps, shape[dim] // blocks).reshape([-1 if axis == dim else 1 for axis in range(len(shape))])
    return factor_of


def scatter_about(key, shape, width, bound, pieces=(), kind=jnp.bfloat16):
    array = jax.random.normal(key, shape, jnp.float32) * width
    if len(pieces) > 0:
        array = levels(key, shape, pieces, -0.22, 0.18) * array
    return jnp.clip(array, min=-bound, max=bound).astype(kind)


def setup_inputs(seed: int = 0) -> dict:
    splits = jax.random.split(jax.random.key(seed), 7)
    return {
        "train_in": scatter_about(splits[0], (NTRAIN, SEQ, DIN), 1.0, 6.0, ((0, 16), (2, 8))),
        "train_grad_out": draw_train_grad_out(jax.random.fold_in(splits[6], 71), 0),
        "target_in": scatter_about(splits[2], (NTGT, SEQ, DIN), 1.0, 6.0, ((0, 16), (2, 8))),
        "target_grad_out": draw_target_grad_out(jax.random.fold_in(splits[6], 71), 0),
        "proj_in": scatter_about(splits[4], (RANK, DIN), DIN ** -0.5, 0.0546875, ((1, 8),)),
        "proj_out": scatter_about(splits[5], (RANK, DOUT), DOUT ** -0.5, 0.09375, ((1, 8),)),
    }


def project(inputs, outputs, proj_in, proj_out):
    def one(pair):
        tokens, grads = pair
        in_proj = jnp.dot(tokens, proj_in.T, preferred_element_type=jnp.float32)
        out_proj = jnp.dot(grads, proj_out.T, preferred_element_type=jnp.float32)
        outer = jnp.dot(out_proj.T, in_proj, precision=lax.Precision.HIGHEST)
        return (outer / inputs.shape[1]).reshape(-1)
    return lax.map(one, (inputs, outputs))


def reference(train_in, train_grad_out, target_in, target_grad_out, proj_in, proj_out):
    train_grads = project(train_in, train_grad_out, proj_in, proj_out)
    target_grads = project(target_in, target_grad_out, proj_in, proj_out)
    trace = jnp.sum(train_grads * train_grads)
    damping = 0.1 * trace / (NTRAIN * RANK * RANK)

    def apply_gram(rows):
        inner = jnp.dot(rows, train_grads.T, precision=lax.Precision.HIGHEST)
        return jnp.dot(inner, train_grads, precision=lax.Precision.HIGHEST) / NTRAIN + damping * rows

    solved = jnp.zeros_like(target_grads)
    residual = target_grads
    direction = target_grads
    norm_now = jnp.sum(residual * residual, axis=1, keepdims=True)
    for step in range(ITERS):
        image = apply_gram(direction)
        alpha = norm_now / jnp.sum(direction * image, axis=1, keepdims=True)
        solved = solved + alpha * direction
        residual = residual - alpha * image
        norm_next = jnp.sum(residual * residual, axis=1, keepdims=True)
        direction = residual + (norm_next / norm_now) * direction
        norm_now = norm_next
    return jnp.dot(train_grads, solved.T, precision=lax.Precision.HIGHEST)
```

```python
import functools

import jax
import jax.numpy as jnp
from jax import lax
from jax.experimental import pallas as pl
from jax.experimental.pallas import tpu as pltpu
from jax.sharding import PartitionSpec as P

MESH = pl.DeviceIdType.MESH
F32 = jnp.float32
BF16 = jnp.bfloat16
ITERS = 4
ND, NM, NX, NZ = 16, 8, 4, 4
NDEV = ND * NM
SEQ, LANES, RANK = 256, 128, 64
ROWS = RANK * RANK // LANES
PAIRS = 8
AHEAD = 6
R1, R2, RAW_A, RAW_B, COMB_A, COMB_B = range(6)


def iota(shape, axis):
    return lax.broadcasted_iota(jnp.int32, shape, axis)


def block_row(rows_ref, tile_ref):
    def body(k, acc):
        tiles = [tile_ref[pl.ds(t * 8 * ROWS + k, 8, stride=ROWS), :] for t in range(2)]
        new = []
        for e in range(NM):
            row = rows_ref[pl.ds(e * ROWS + k, 1), :]
            for t in range(2):
                new.append(acc[e * 2 + t] + tiles[t] * row)
        return tuple(new)

    acc = lax.fori_loop(0, ROWS, body, tuple(jnp.zeros((8, LANES), F32) for _ in range(2 * NM)), unroll=4)
    lane, sub = iota((8, LANES), 1), iota((8, LANES), 0)
    spread = jnp.zeros((8, LANES), F32)
    for i in range(2 * NM):
        spread = jnp.where(lane // 8 == i, jnp.sum(acc[i], axis=1, keepdims=True), spread)
    return jnp.sum(jnp.where(lane % 8 == sub, spread, 0.0), axis=0, keepdims=True)


def swap_blocks(tile):
    diag = iota((8, LANES), 1) // 16 == iota((8, LANES), 0)
    out = jnp.where(diag, tile, 0.0)
    for s in range(1, 8):
        moved = jnp.where(diag, pltpu.roll(tile, s * 16, 1), 0.0)
        out = out + pltpu.roll(moved, 8 - s, 0)
    return out


def gradient(out_part, in_part):
    outer = lax.dot_general(
        out_part, in_part, (((1,), (1,)), ((), ())), precision=lax.Precision.HIGHEST, preferred_element_type=F32
    )
    return jnp.concatenate([outer[: RANK // 2, :], outer[RANK // 2 :, :]], axis=1) * (1.0 / SEQ)


def kernel(
    train_in, train_go, target_in, target_go, proj_in, proj_out, out_ref,
    xin, xgo, w_in, w_out, part, sibr, rsr, t_own, b_own, t_m, t_g, b_g, msg, fin, c_mat, k_mat,
    in_sem, w_sem, sib_ss, sib_rs, rs_ss, rs_rs, t_ss, t_rs, b_ss, b_rs, f_ss, f_rs, xsem,
):
    dp, mp = lax.axis_index("dp"), lax.axis_index("mp")
    y, x, z, c = dp // NX, dp % NX, mp // 2, mp % 2
    zp, zm = ((z + 1) % NZ) * 2 + c, ((z + 3) % NZ) * 2 + c

    def item_copies(s, source_in, source_go):
        kidx, mine = (s // 2) % 4, s % 2
        k = (2 + 3 * kidx + 3 * (kidx // 2) + 2 * (kidx // 3)) % 4
        e = ((z + k) % NZ) * 2 + (c + 1 - mine) % 2
        return (
            pltpu.make_async_copy(source_in.at[e], xin.at[s], in_sem.at[s, 0]),
            pltpu.make_async_copy(source_go.at[e], xgo.at[s], in_sem.at[s, 1]),
        )

    def start_item(s):
        @pl.when(s < PAIRS)
        def _():
            for copy in item_copies(s, train_in, train_go):
                copy.start()

        @pl.when((s >= PAIRS) & (s < 2 * PAIRS))
        def _():
            for copy in item_copies(s, target_in, target_go):
                copy.start()

    w_copies = (
        pltpu.make_async_copy(proj_in, w_in, w_sem.at[0]),
        pltpu.make_async_copy(proj_out, w_out, w_sem.at[1]),
    )
    for copy in w_copies:
        copy.start()
    for s in range(AHEAD):
        start_item(s)

    bar = pltpu.get_barrier_semaphore()
    for o in range(1, NM):
        pl.semaphore_signal(bar, inc=1, device_id=(dp, (mp + o) % NM), device_id_type=MESH)
    for o in range(1, 4):
        pl.semaphore_signal(bar, inc=1, device_id=(y * NX + (x + o) % NX, mp), device_id_type=MESH)
        pl.semaphore_signal(bar, inc=1, device_id=(((y + o) % 4) * NX + x, mp), device_id_type=MESH)

    for copy in w_copies:
        copy.wait()

    def project(s):
        for copy in item_copies(s, train_in, train_go):
            copy.wait()
        part[s, :RANK, :] = lax.dot_general(w_out[...], xgo[s], (((1,), (1,)), ((), ())), preferred_element_type=F32)
        part[s, RANK:, :] = jnp.dot(w_in[...], xin[s], preferred_element_type=F32)

    def sib_copy(q):
        return pltpu.make_async_remote_copy(
            src_ref=part.at[2 * q], dst_ref=sibr.at[q], send_sem=sib_ss, recv_sem=sib_rs.at[q],
            device_id=(dp, z * 2 + (1 - c)), device_id_type=MESH,
        )

    def ring_copy(src, ph, slot, to):
        return pltpu.make_async_remote_copy(
            src_ref=src, dst_ref=rsr.at[ph * 6 + slot], send_sem=rs_ss, recv_sem=rs_rs.at[ph * 6 + slot],
            device_id=(dp, to), device_id_type=MESH,
        )

    low, high = pl.ds(0, RANK), pl.ds(RANK, RANK)

    def merge(q):
        sib_copy(q).wait_recv()
        s, ph, kidx = 2 * q + 1, q // 4, q % 4
        part[s] = part[s] + sibr[q]

        @pl.when(kidx == 0)
        def _():
            ring_copy(part.at[s, low], ph, R1, zp).start()
            ring_copy(part.at[s, high], ph, R2, zm).start()

        @pl.when(kidx == 1)
        def _():
            ring_copy(part.at[s, high], ph, RAW_B, zp).start()

        @pl.when(kidx == 2)
        def _():
            ring_copy(part.at[s, low], ph, RAW_A, zm).start()

    project(0)
    project(1)
    pl.semaphore_wait(bar, NM - 1 + 6)
    sib_copy(0).start()
    for o in range(1, 4):
        pl.semaphore_signal(xsem, inc=1, device_id=(y * NX + (x + o) % NX, mp), device_id_type=MESH)
    start_item(AHEAD)
    start_item(AHEAD + 1)

    def pair(q, carry):
        project(2 * q)
        sib_copy(q).start()
        project(2 * q + 1)
        start_item(2 * q + AHEAD)
        start_item(2 * q + 1 + AHEAD)
        merge(q - 1)
        return carry

    lax.fori_loop(1, PAIRS, pair, 0)
    merge(PAIRS - 1)

    def forward(ph):
        s_next, s_prev = 2 * (4 * ph + 1) + 1, 2 * (4 * ph + 2) + 1
        ring_copy(part.at[s_next, low], ph, R1, zp).wait_recv()
        part[s_next, :RANK, :] = part[s_next, :RANK, :] + rsr[ph * 6 + R1]
        ring_copy(part.at[s_next, low], ph, COMB_A, zp).start()
        ring_copy(part.at[s_prev, high], ph, R2, zm).wait_recv()
        part[s_prev, RANK:, :] = part[s_prev, RANK:, :] + rsr[ph * 6 + R2]
        ring_copy(part.at[s_prev, high], ph, COMB_B, zm).start()

    def finish(ph):
        s = 2 * (4 * ph + 3) + 1
        for slot in (RAW_A, RAW_B, COMB_A, COMB_B):
            ring_copy(part.at[s, low], ph, slot, zp).wait_recv()
        top = part[s, :RANK, :] + rsr[ph * 6 + RAW_A] + rsr[ph * 6 + COMB_A]
        bottom = part[s, RANK:, :] + rsr[ph * 6 + RAW_B] + rsr[ph * 6 + COMB_B]
        return gradient(top, bottom)

    forward(0)
    forward(1)

    own_d, own_m = pl.ds(pl.multiple_of(dp * ROWS, ROWS), ROWS), pl.ds(pl.multiple_of(mp * ROWS, ROWS), ROWS)

    def mp_copy(o, src, dst, ss, rs):
        return pltpu.make_async_remote_copy(
            src_ref=src, dst_ref=dst.at[own_m], send_sem=ss, recv_sem=rs, device_id=(dp, (mp + o) % NM), device_id_type=MESH
        )

    def dp_copy(o, src, dst, ss, rs):
        return pltpu.make_async_remote_copy(
            src_ref=src, dst_ref=dst.at[own_d], send_sem=ss, recv_sem=rs, device_id=((dp + o) % ND, mp), device_id_type=MESH
        )

    train_row = finish(0)
    t_own[...] = train_row
    pl.semaphore_wait(xsem, 3)
    for o in range(1, ND):
        dp_copy(o, t_own, t_m, t_ss.at[0], t_rs.at[0]).start()
    for o in range(1, NM):
        mp_copy(o, t_own, t_g, t_ss.at[1], t_rs.at[1]).start()
    t_m[own_d, :] = train_row
    t_g[own_m, :] = train_row

    target_row = finish(1)
    b_own[...] = target_row
    for o in range(1, NM):
        mp_copy(o, b_own, b_g, b_ss, b_rs).start()
    b_g[own_m, :] = target_row
    msg[2:3, :] = jnp.broadcast_to(jnp.sum(target_row * target_row), (1, LANES))
    msg[3:4, :] = jnp.zeros((1, LANES), F32)

    def bytes_of(ref, sem):
        return pltpu.make_async_copy(ref, ref, sem)

    dp_rest, mp_rest = pl.ds(0, (ND - 1) * ROWS), pl.ds(0, (NM - 1) * ROWS)
    bytes_of(t_m.at[dp_rest], t_rs.at[0]).wait()
    bytes_of(t_g.at[mp_rest], t_rs.at[1]).wait()
    msg[1:2, :] = block_row(t_g, t_m)
    bytes_of(b_g.at[mp_rest], b_rs).wait()
    msg[0:1, :] = block_row(b_g, t_m)

    me = dp * NM + mp

    def send_all(o, carry):
        to_y, to_x = (y + 2 + o // 32) % 4, (x + 2 + (o // 8) % 4) % 4
        to_z, to_c = (z + 2 + (o // 2) % 4) % 4, (c + 1 + o) % 2
        to_dp, to_mp = to_y * NX + to_x, to_z * 2 + to_c

        @pl.when(to_dp * NM + to_mp != me)
        def _():
            pltpu.make_async_remote_copy(
                src_ref=msg, dst_ref=fin.at[me], send_sem=f_ss, recv_sem=f_rs, device_id=(to_dp, to_mp), device_id_type=MESH
            ).start()

        return carry

    lax.fori_loop(0, NDEV, send_all, 0)
    fin[me] = msg[...]
    bytes_of(fin.at[pl.ds(0, NDEV - 1)], f_rs).wait()

    for d in range(ND):
        rows = pl.ds(d * NM, NM)
        c_mat[rows, :] = swap_blocks(fin[rows, 0, :])
        k_mat[pl.ds(d, NM, stride=ND), :] = swap_blocks(fin[rows, 1, :])
    norm = fin[:, 2, :][:, :1]

    gram = k_mat[...]
    lane, sub = iota((NDEV, LANES), 1), iota((NDEV, LANES), 0)
    trace = jnp.sum(jnp.where(lane == sub, gram, 0.0), keepdims=True)
    damping = trace * (0.1 / (NDEV * RANK * RANK))
    inv = 1.0 / NDEV
    u_res = c_mat[...]
    u_dir, scores, dir_norm = u_res, jnp.zeros_like(u_res), norm
    for step in range(ITERS):
        u_norm = jnp.sum(u_dir * u_dir, axis=1, keepdims=True)
        alpha = norm / (damping * dir_norm + u_norm * inv)
        scores = scores + alpha * u_dir
        if step == ITERS - 1:
            break
        image = lax.dot_general(u_dir, gram, (((1,), (0,)), ((), ())), precision=lax.Precision.HIGHEST, preferred_element_type=F32)
        u_gram = jnp.sum(u_dir * image, axis=1, keepdims=True)
        squared = damping * damping * dir_norm + 2.0 * inv * damping * u_norm + inv * inv * u_gram
        following = alpha * alpha * squared - norm
        u_res = u_res - alpha * (damping * u_dir + inv * image)
        ratio = following / norm
        u_dir = u_res + ratio * u_dir
        dir_norm = following + ratio * ratio * dir_norm
        norm = following
    column = jnp.sum(jnp.where(lane == mp * ND + dp, scores, 0.0), axis=1, keepdims=True)
    out_ref[...] = jnp.sum(jnp.where(lane == sub, column, 0.0), axis=0, keepdims=True)

    bytes_of(part.at[pl.ds(0, PAIRS)], sib_ss).wait()
    bytes_of(rsr, rs_ss).wait()
    bytes_of(t_m.at[dp_rest], t_ss.at[0]).wait()
    bytes_of(t_g.at[mp_rest], t_ss.at[1]).wait()
    bytes_of(b_g.at[mp_rest], b_ss).wait()
    bytes_of(fin.at[pl.ds(0, NDEV - 1)], f_ss).wait()


def local(train_in, train_grad_out, target_in, target_grad_out, proj_in, proj_out):
    d_in, d_out = proj_in.shape[1], proj_out.shape[1]
    dma, vmem = pltpu.SemaphoreType.DMA, pltpu.VMEM
    return pl.pallas_call(
        kernel,
        out_shape=jax.ShapeDtypeStruct((1, NDEV), F32),
        in_specs=[pl.BlockSpec(memory_space=pltpu.HBM)] * 6,
        out_specs=pl.BlockSpec(memory_space=pltpu.VMEM),
        scratch_shapes=[
            vmem((2 * PAIRS, d_in, SEQ), BF16),
            vmem((2 * PAIRS, SEQ, d_out), BF16),
            vmem((RANK, d_in), BF16),
            vmem((RANK, d_out), BF16),
            vmem((2 * PAIRS, 2 * RANK, SEQ), F32),
            vmem((PAIRS, 2 * RANK, SEQ), F32),
            vmem((12, RANK, SEQ), F32),
            vmem((ROWS, LANES), F32),
            vmem((ROWS, LANES), F32),
            vmem((ND * ROWS, LANES), F32),
            vmem((NM * ROWS, LANES), F32),
            vmem((NM * ROWS, LANES), F32),
            vmem((4, LANES), F32),
            vmem((NDEV, 4, LANES), F32),
            vmem((NDEV, LANES), F32),
            vmem((NDEV, LANES), F32),
            dma((2 * PAIRS, 2)),
            dma((2,)),
            dma,
            dma((PAIRS,)),
            dma,
            dma((12,)),
            dma((2,)),
            dma((2,)),
            dma,
            dma,
            dma,
            dma,
            pltpu.SemaphoreType.REGULAR,
        ],
        compiler_params=pltpu.CompilerParams(collective_id=0, has_side_effects=True, vmem_limit_bytes=60 * 1024 * 1024),
    )(train_in.swapaxes(1, 2), train_grad_out, target_in.swapaxes(1, 2), target_grad_out, proj_in, proj_out)


def solution(mesh):
    return jax.shard_map(
        local,
        mesh=mesh,
        in_specs=(
            P("dp", None, "mp"),
            P("dp", None, "mp"),
            P("dp", None, "mp"),
            P("dp", None, "mp"),
            P(None, "mp"),
            P(None, "mp"),
        ),
        out_specs=P(("dp", "mp"), None),
        check_vma=False,
    )
```

```python
import functools

import jax
import jax.numpy as jnp
from jax import lax
from jax.experimental import pallas as pl
from jax.experimental.pallas import tpu as pltpu
from jax.sharding import PartitionSpec as P

MESH = pl.DeviceIdType.MESH
F32 = jnp.float32
BF16 = jnp.bfloat16
ITERS = 4
ND, NM, NX, NZ = 16, 8, 4, 4
NDEV = ND * NM
SEQ, LANES, RANK = 256, 128, 64
ROWS = RANK * RANK // LANES
PAIRS = 8
AHEAD = 6
LAG = 2
FORWARD_AT = 6
ORDER = ((0, 2), (1, 2), (0, 1), (0, 3), (1, 1), (1, 3), (0, 0), (1, 0))
PHASE_BITS = sum(ph << q for q, (ph, _) in enumerate(ORDER))
CHIP_BITS = sum(k << 2 * q for q, (_, k) in enumerate(ORDER))
R1, R2, RAW_A, RAW_B, COMB_A, COMB_B = range(6)


def iota(shape, axis):
    return lax.broadcasted_iota(jnp.int32, shape, axis)


def block_row(rows_ref, tile_ref):
    def body(k, acc):
        tiles = [tile_ref[pl.ds(t * 8 * ROWS + k, 8, stride=ROWS), :] for t in range(2)]
        new = []
        for e in range(NM):
            row = rows_ref[pl.ds(e * ROWS + k, 1), :]
            for t in range(2):
                new.append(acc[e * 2 + t] + tiles[t] * row)
        return tuple(new)

    acc = lax.fori_loop(0, ROWS, body, tuple(jnp.zeros((8, LANES), F32) for _ in range(2 * NM)), unroll=4)
    lane, sub = iota((8, LANES), 1), iota((8, LANES), 0)
    spread = jnp.zeros((8, LANES), F32)
    for i in range(2 * NM):
        spread = jnp.where(lane // 8 == i, jnp.sum(acc[i], axis=1, keepdims=True), spread)
    return jnp.sum(jnp.where(lane % 8 == sub, spread, 0.0), axis=0, keepdims=True)


def swap_blocks(tile):
    diag = iota((8, LANES), 1) // 16 == iota((8, LANES), 0)
    out = jnp.where(diag, tile, 0.0)
    for s in range(1, 8):
        moved = jnp.where(diag, pltpu.roll(tile, s * 16, 1), 0.0)
        out = out + pltpu.roll(moved, 8 - s, 0)
    return out


def gradient(out_part, in_part):
    outer = lax.dot_general(
        out_part, in_part, (((1,), (1,)), ((), ())), precision=lax.Precision.HIGHEST, preferred_element_type=F32
    )
    return jnp.concatenate([outer[: RANK // 2, :], outer[RANK // 2 :, :]], axis=1) * (1.0 / SEQ)


def kernel(
    train_in, train_go, target_in, target_go, proj_in, proj_out, out_ref,
    xin, xgo, w_in, w_out, part, sibr, rsr, t_own, b_own, t_m, t_g, b_g, msg, fin, c_mat, k_mat,
    in_sem, w_sem, sib_ss, sib_rs, rs_ss, rs_rs, t_ss, t_rs, b_ss, b_rs, f_ss, f_rs, xsem,
):
    dp, mp = lax.axis_index("dp"), lax.axis_index("mp")
    y, x, z, c = dp // NX, dp % NX, mp // 2, mp % 2
    zp, zm = ((z + 1) % NZ) * 2 + c, ((z + 3) % NZ) * 2 + c

    def item_copies(s, source_in, source_go):
        k = lax.shift_right_logical(CHIP_BITS, 2 * (s // 2)) & 3
        e = ((z + k) % NZ) * 2 + (c + 1 + s) % 2
        return (
            pltpu.make_async_copy(source_in.at[e], xin.at[s], in_sem.at[s, 0]),
            pltpu.make_async_copy(source_go.at[e], xgo.at[s], in_sem.at[s, 1]),
        )

    def start_item(s):
        phase = lax.shift_right_logical(PHASE_BITS, s // 2) & 1

        @pl.when((phase == 0) & (s < 2 * PAIRS))
        def _():
            for copy in item_copies(s, train_in, train_go):
                copy.start()

        @pl.when((phase == 1) & (s < 2 * PAIRS))
        def _():
            for copy in item_copies(s, target_in, target_go):
                copy.start()

    w_copies = (
        pltpu.make_async_copy(proj_in, w_in, w_sem.at[0]),
        pltpu.make_async_copy(proj_out, w_out, w_sem.at[1]),
    )
    for copy in w_copies:
        copy.start()
    for s in range(2):
        start_item(s)

    bar = pltpu.get_barrier_semaphore()
    for o in range(1, NM):
        pl.semaphore_signal(bar, inc=1, device_id=(dp, (mp + o) % NM), device_id_type=MESH)
    for o in range(1, 4):
        pl.semaphore_signal(bar, inc=1, device_id=(y * NX + (x + o) % NX, mp), device_id_type=MESH)
        pl.semaphore_signal(bar, inc=1, device_id=(((y + o) % 4) * NX + x, mp), device_id_type=MESH)

    for copy in w_copies:
        copy.wait()
    for s in range(2, AHEAD):
        start_item(s)

    def project(s):
        for copy in item_copies(s, train_in, train_go):
            copy.wait()
        part[s, :RANK, :] = lax.dot_general(w_out[...], xgo[s], (((1,), (1,)), ((), ())), preferred_element_type=F32)
        part[s, RANK:, :] = jnp.dot(w_in[...], xin[s], preferred_element_type=F32)

    def sib_copy(q):
        return pltpu.make_async_remote_copy(
            src_ref=part.at[2 * q], dst_ref=sibr.at[q], send_sem=sib_ss, recv_sem=sib_rs.at[q],
            device_id=(dp, z * 2 + (1 - c)), device_id_type=MESH,
        )

    def ring_copy(src, ph, slot, to):
        return pltpu.make_async_remote_copy(
            src_ref=src, dst_ref=rsr.at[ph * 6 + slot], send_sem=rs_ss, recv_sem=rs_rs.at[ph * 6 + slot],
            device_id=(dp, to), device_id_type=MESH,
        )

    low, high = pl.ds(0, RANK), pl.ds(RANK, RANK)

    def merge(q):
        sib_copy(q).wait_recv()
        s = 2 * q + 1
        part[s] = part[s] + sibr[q]
        for j, (ph, k) in enumerate(ORDER):

            @pl.when(q == j)
            def _():
                if k == 2:
                    ring_copy(part.at[s, low], ph, R1, zp).start()
                    ring_copy(part.at[s, high], ph, R2, zm).start()
                if k == 1:
                    ring_copy(part.at[s, high], ph, RAW_B, zp).start()
                if k == 3:
                    ring_copy(part.at[s, low], ph, RAW_A, zm).start()

    def slot_of(ph, k):
        return 2 * ORDER.index((ph, k)) + 1

    def forward(ph):
        s_next, s_prev = slot_of(ph, 1), slot_of(ph, 3)
        ring_copy(part.at[s_next, low], ph, R1, zp).wait_recv()
        part[s_next, :RANK, :] = part[s_next, :RANK, :] + rsr[ph * 6 + R1]
        ring_copy(part.at[s_next, low], ph, COMB_A, zp).start()
        ring_copy(part.at[s_prev, high], ph, R2, zm).wait_recv()
        part[s_prev, RANK:, :] = part[s_prev, RANK:, :] + rsr[ph * 6 + R2]
        ring_copy(part.at[s_prev, high], ph, COMB_B, zm).start()

    def finish(ph):
        s = slot_of(ph, 0)
        for slot in (RAW_A, RAW_B, COMB_A, COMB_B):
            ring_copy(part.at[s, low], ph, slot, zp).wait_recv()
        top = part[s, :RANK, :] + rsr[ph * 6 + RAW_A] + rsr[ph * 6 + COMB_A]
        bottom = part[s, RANK:, :] + rsr[ph * 6 + RAW_B] + rsr[ph * 6 + COMB_B]
        return gradient(top, bottom)

    project(0)
    project(1)
    pl.semaphore_wait(bar, NM - 1 + 6)
    sib_copy(0).start()
    for o in range(1, 4):
        pl.semaphore_signal(xsem, inc=1, device_id=(y * NX + (x + o) % NX, mp), device_id_type=MESH)
    start_item(AHEAD)
    start_item(AHEAD + 1)

    def pair(q, carry):
        project(2 * q)
        sib_copy(q).start()
        project(2 * q + 1)
        start_item(2 * q + AHEAD)
        start_item(2 * q + 1 + AHEAD)
        @pl.when(q >= LAG)
        def _():
            merge(q - LAG)

        @pl.when(q == FORWARD_AT)
        def _():
            forward(0)

        return carry

    lax.fori_loop(1, PAIRS, pair, 0)
    for q in range(PAIRS - LAG, PAIRS):
        merge(q)
    forward(1)

    own_d, own_m = pl.ds(pl.multiple_of(dp * ROWS, ROWS), ROWS), pl.ds(pl.multiple_of(mp * ROWS, ROWS), ROWS)

    def mp_copy(o, src, dst, ss, rs):
        return pltpu.make_async_remote_copy(
            src_ref=src, dst_ref=dst.at[own_m], send_sem=ss, recv_sem=rs, device_id=(dp, (mp + o) % NM), device_id_type=MESH
        )

    def dp_copy(o, src, dst, ss, rs):
        return pltpu.make_async_remote_copy(
            src_ref=src, dst_ref=dst.at[own_d], send_sem=ss, recv_sem=rs, device_id=((dp + o) % ND, mp), device_id_type=MESH
        )

    train_row = finish(0)
    t_own[...] = train_row
    pl.semaphore_wait(xsem, 3)
    for o in range(1, ND):
        dp_copy(o, t_own, t_m, t_ss.at[0], t_rs.at[0]).start()
    for o in range(1, NM):
        mp_copy(o, t_own, t_g, t_ss.at[1], t_rs.at[1]).start()
    t_m[own_d, :] = train_row
    t_g[own_m, :] = train_row

    target_row = finish(1)
    b_own[...] = target_row
    for o in range(1, NM):
        mp_copy(o, b_own, b_g, b_ss, b_rs).start()
    b_g[own_m, :] = target_row
    msg[2:3, :] = jnp.broadcast_to(jnp.sum(target_row * target_row), (1, LANES))

    def bytes_of(ref, sem):
        return pltpu.make_async_copy(ref, ref, sem)

    dp_rest, mp_rest = pl.ds(0, (ND - 1) * ROWS), pl.ds(0, (NM - 1) * ROWS)
    bytes_of(t_m.at[dp_rest], t_rs.at[0]).wait()
    bytes_of(t_g.at[mp_rest], t_rs.at[1]).wait()
    msg[1:2, :] = block_row(t_g, t_m)
    bytes_of(b_g.at[mp_rest], b_rs).wait()
    msg[0:1, :] = block_row(b_g, t_m)

    me = dp * NM + mp

    to_dps = [((y + dy) % 4) * NX + (x + dx) % NX for dy in (2, 1, 3, 0) for dx in (2, 1, 3, 0)]
    to_mps = [((z + dz) % NZ) * 2 + (c + dc) % 2 for dz in (2, 1, 3, 0) for dc in (1, 0)]
    for to in [(to_dp, to_mp) for to_dp in to_dps for to_mp in to_mps][:-1]:
        pltpu.make_async_remote_copy(
            src_ref=msg, dst_ref=fin.at[me], send_sem=f_ss, recv_sem=f_rs, device_id=to, device_id_type=MESH
        ).start()
    fin[me] = msg[...]
    bytes_of(fin.at[pl.ds(0, NDEV - 1)], f_rs).wait()

    for d in range(ND):
        rows = pl.ds(d * NM, NM)
        c_mat[rows, :] = swap_blocks(fin[rows, 0, :])
        k_mat[pl.ds(d, NM, stride=ND), :] = swap_blocks(fin[rows, 1, :])
    norm = fin[:, 2, :][:, :1]

    gram = k_mat[...]
    lane, sub = iota((NDEV, LANES), 1), iota((NDEV, LANES), 0)
    trace = jnp.sum(jnp.where(lane == sub, gram, 0.0), keepdims=True)
    damping = trace * (0.1 / (NDEV * RANK * RANK))
    inv = 1.0 / NDEV
    u_res = c_mat[...]
    u_dir, scores, dir_norm = u_res, jnp.zeros_like(u_res), norm
    for step in range(ITERS):
        u_norm = jnp.sum(u_dir * u_dir, axis=1, keepdims=True)
        alpha = norm / (damping * dir_norm + u_norm * inv)
        scores = scores + alpha * u_dir
        if step == ITERS - 1:
            break
        image = lax.dot_general(u_dir, gram, (((1,), (0,)), ((), ())), precision=lax.Precision.HIGHEST, preferred_element_type=F32)
        u_gram = jnp.sum(u_dir * image, axis=1, keepdims=True)
        squared = damping * damping * dir_norm + 2.0 * inv * damping * u_norm + inv * inv * u_gram
        following = alpha * alpha * squared - norm
        u_res = u_res - alpha * (damping * u_dir + inv * image)
        ratio = following / norm
        u_dir = u_res + ratio * u_dir
        dir_norm = following + ratio * ratio * dir_norm
        norm = following
    column = jnp.sum(jnp.where(lane == mp * ND + dp, scores, 0.0), axis=1, keepdims=True)
    spread = jnp.where(lane == sub, column, 0.0)
    out_ref[...] = sum(spread[8 * d : 8 * d + 8, :] for d in range(ND))

    bytes_of(part.at[pl.ds(0, PAIRS)], sib_ss).wait()
    bytes_of(rsr, rs_ss).wait()
    bytes_of(t_m.at[dp_rest], t_ss.at[0]).wait()
    bytes_of(t_g.at[mp_rest], t_ss.at[1]).wait()
    bytes_of(b_g.at[mp_rest], b_ss).wait()
    bytes_of(fin.at[pl.ds(0, NDEV - 1)], f_ss).wait()


def local(train_in, train_grad_out, target_in, target_grad_out, proj_in, proj_out):
    d_in, d_out = proj_in.shape[1], proj_out.shape[1]
    dma, vmem = pltpu.SemaphoreType.DMA, pltpu.VMEM
    spread = pl.pallas_call(
        kernel,
        out_shape=jax.ShapeDtypeStruct((8, NDEV), F32),
        in_specs=[pl.BlockSpec(memory_space=pltpu.HBM)] * 6,
        out_specs=pl.BlockSpec(memory_space=pltpu.VMEM),
        scratch_shapes=[
            vmem((2 * PAIRS, d_in, SEQ), BF16),
            vmem((2 * PAIRS, SEQ, d_out), BF16),
            vmem((RANK, d_in), BF16),
            vmem((RANK, d_out), BF16),
            vmem((2 * PAIRS, 2 * RANK, SEQ), F32),
            vmem((PAIRS, 2 * RANK, SEQ), F32),
            vmem((12, RANK, SEQ), F32),
            vmem((ROWS, LANES), F32),
            vmem((ROWS, LANES), F32),
            vmem((ND * ROWS, LANES), F32),
            vmem((NM * ROWS, LANES), F32),
            vmem((NM * ROWS, LANES), F32),
            vmem((3, LANES), F32),
            vmem((NDEV, 3, LANES), F32),
            vmem((NDEV, LANES), F32),
            vmem((NDEV, LANES), F32),
            dma((2 * PAIRS, 2)),
            dma((2,)),
            dma,
            dma((PAIRS,)),
            dma,
            dma((12,)),
            dma((2,)),
            dma((2,)),
            dma,
            dma,
            dma,
            dma,
            pltpu.SemaphoreType.REGULAR,
        ],
        compiler_params=pltpu.CompilerParams(collective_id=0, has_side_effects=True, vmem_limit_bytes=32 * 1024 * 1024),
    )(*(
        pltpu.with_memory_space_constraint(a, pltpu.HBM)
        for a in (train_in.swapaxes(1, 2), train_grad_out, target_in.swapaxes(1, 2), target_grad_out, proj_in, proj_out)
    ))
    return jnp.sum(spread, axis=0, keepdims=True)


def solution(mesh):
    return jax.shard_map(
        local,
        mesh=mesh,
        in_specs=(
            P("dp", None, "mp"),
            P("dp", None, "mp"),
            P("dp", None, "mp"),
            P("dp", None, "mp"),
            P(None, "mp"),
            P(None, "mp"),
        ),
        out_specs=P(("dp", "mp"), None),
        check_vma=False,
    )
```

```python
import functools

import jax
import jax.numpy as jnp
from jax import lax
from jax.experimental import pallas as pl
from jax.experimental.pallas import tpu as pltpu
from jax.sharding import PartitionSpec as P

MESH = pl.DeviceIdType.MESH
F32 = jnp.float32
BF16 = jnp.bfloat16
ITERS = 4
ND, NM, NX, NZ = 16, 8, 4, 4
NDEV = ND * NM
SEQ, LANES, RANK = 256, 128, 64
ROWS = RANK * RANK // LANES
PAIRS = 8
AHEAD = 6
LAG = 2
FORWARD_AT = 5
ORDER = ((0, 2), (1, 2), (0, 1), (0, 3), (1, 1), (1, 3), (0, 0), (1, 0))
PHASE_BITS = sum(ph << q for q, (ph, _) in enumerate(ORDER))
CHIP_BITS = sum(k << 2 * q for q, (_, k) in enumerate(ORDER))
R1, R2, RAW_A, RAW_B, COMB_A, COMB_B = range(6)


def iota(shape, axis):
    return lax.broadcasted_iota(jnp.int32, shape, axis)


def block_row(rows_ref, tile_ref):
    def body(k, acc):
        tiles = [tile_ref[pl.ds(t * 8 * ROWS + k, 8, stride=ROWS), :] for t in range(2)]
        new = []
        for e in range(NM):
            row = rows_ref[pl.ds(e * ROWS + k, 1), :]
            for t in range(2):
                new.append(acc[e * 2 + t] + tiles[t] * row)
        return tuple(new)

    acc = lax.fori_loop(0, ROWS, body, tuple(jnp.zeros((8, LANES), F32) for _ in range(2 * NM)), unroll=4)
    lane, sub = iota((8, LANES), 1), iota((8, LANES), 0)
    spread = jnp.zeros((8, LANES), F32)
    for i in range(2 * NM):
        spread = jnp.where(lane // 8 == i, jnp.sum(acc[i], axis=1, keepdims=True), spread)
    return jnp.sum(jnp.where(lane % 8 == sub, spread, 0.0), axis=0, keepdims=True)


def swap_blocks(tile):
    diag = iota((8, LANES), 1) // 16 == iota((8, LANES), 0)
    out = jnp.where(diag, tile, 0.0)
    for s in range(1, 8):
        moved = jnp.where(diag, pltpu.roll(tile, s * 16, 1), 0.0)
        out = out + pltpu.roll(moved, 8 - s, 0)
    return out


def gradient(out_part, in_part):
    outer = lax.dot_general(
        out_part, in_part, (((1,), (1,)), ((), ())), precision=lax.Precision.HIGHEST, preferred_element_type=F32
    )
    return jnp.concatenate([outer[: RANK // 2, :], outer[RANK // 2 :, :]], axis=1) * (1.0 / SEQ)


def kernel(
    train_in, train_go, target_in, target_go, proj_in, proj_out, out_ref,
    xin, xgo, w_in, w_out, part, sibr, rsr, t_own, b_own, t_m, t_g, b_g, msg, fin, c_mat, k_mat,
    in_sem, w_sem, sib_ss, sib_rs, rs_ss, rs_rs, t_ss, t_rs, b_ss, b_rs, f_ss, f_rs, xsem,
):
    dp, mp = lax.axis_index("dp"), lax.axis_index("mp")
    y, x, z, c = dp // NX, dp % NX, mp // 2, mp % 2
    zp, zm = ((z + 1) % NZ) * 2 + c, ((z + 3) % NZ) * 2 + c

    def item_copies(s, source_in, source_go):
        k = lax.shift_right_logical(CHIP_BITS, 2 * (s // 2)) & 3
        e = ((z + k) % NZ) * 2 + (c + 1 + s) % 2
        return (
            pltpu.make_async_copy(source_in.at[e], xin.at[s], in_sem.at[s, 0]),
            pltpu.make_async_copy(source_go.at[e], xgo.at[s], in_sem.at[s, 1]),
        )

    def start_item(s):
        phase = lax.shift_right_logical(PHASE_BITS, s // 2) & 1

        @pl.when((phase == 0) & (s < 2 * PAIRS))
        def _():
            for copy in item_copies(s, train_in, train_go):
                copy.start()

        @pl.when((phase == 1) & (s < 2 * PAIRS))
        def _():
            for copy in item_copies(s, target_in, target_go):
                copy.start()

    w_copies = (pltpu.make_async_copy(proj_out, w_out, w_sem.at[0]), pltpu.make_async_copy(proj_in, w_in, w_sem.at[1]))
    first = [item_copies(s, train_in, train_go) for s in range(2)]
    w_copies[0].start()
    for copies in first:
        copies[1].start()
    w_copies[1].start()
    for copies in first:
        copies[0].start()

    bar = pltpu.get_barrier_semaphore()
    for o in range(1, NM):
        pl.semaphore_signal(bar, inc=1, device_id=(dp, (mp + o) % NM), device_id_type=MESH)
    for o in range(1, 4):
        pl.semaphore_signal(bar, inc=1, device_id=(y * NX + (x + o) % NX, mp), device_id_type=MESH)
        pl.semaphore_signal(bar, inc=1, device_id=(((y + o) % 4) * NX + x, mp), device_id_type=MESH)

    def project_out(s):
        item_copies(s, train_in, train_go)[1].wait()
        part[s, :RANK, :] = lax.dot_general(w_out[...], xgo[s], (((1,), (1,)), ((), ())), preferred_element_type=F32)

    def project_in(s):
        item_copies(s, train_in, train_go)[0].wait()
        part[s, RANK:, :] = jnp.dot(w_in[...], xin[s], preferred_element_type=F32)

    def project(s):
        for copy in item_copies(s, train_in, train_go):
            copy.wait()
        part[s, :RANK, :] = lax.dot_general(w_out[...], xgo[s], (((1,), (1,)), ((), ())), preferred_element_type=F32)
        part[s, RANK:, :] = jnp.dot(w_in[...], xin[s], preferred_element_type=F32)

    low, high = pl.ds(0, RANK), pl.ds(RANK, RANK)

    def sib_half(half, sem):
        return pltpu.make_async_remote_copy(
            src_ref=part.at[0, half], dst_ref=sibr.at[0, half], send_sem=sib_ss, recv_sem=sib_rs.at[sem],
            device_id=(dp, z * 2 + (1 - c)), device_id_type=MESH,
        )

    def project_pair(q):
        for s in (2 * q, 2 * q + 1):
            for copy in item_copies(s, train_in, train_go):
                copy.wait()
        for s in (2 * q, 2 * q + 1):
            part[s, :RANK, :] = lax.dot_general(w_out[...], xgo[s], (((1,), (1,)), ((), ())), preferred_element_type=F32)
            part[s, RANK:, :] = jnp.dot(w_in[...], xin[s], preferred_element_type=F32)

    def sib_copy(q):
        return pltpu.make_async_remote_copy(
            src_ref=part.at[2 * q], dst_ref=sibr.at[q], send_sem=sib_ss, recv_sem=sib_rs.at[q],
            device_id=(dp, z * 2 + (1 - c)), device_id_type=MESH,
        )

    def ring_copy(src, ph, slot, to):
        return pltpu.make_async_remote_copy(
            src_ref=src, dst_ref=rsr.at[ph * 6 + slot], send_sem=rs_ss, recv_sem=rs_rs.at[ph * 6 + slot],
            device_id=(dp, to), device_id_type=MESH,
        )

    def merge(q):
        sib_copy(q).wait_recv()
        s = 2 * q + 1
        part[s] = part[s] + sibr[q]
        for j, (ph, k) in list(enumerate(ORDER))[1:]:

            @pl.when(q == j)
            def _():
                if k == 2:
                    ring_copy(part.at[s, low], ph, R1, zp).start()
                    ring_copy(part.at[s, high], ph, R2, zm).start()
                if k == 1:
                    ring_copy(part.at[s, high], ph, RAW_B, zp).start()
                if k == 3:
                    ring_copy(part.at[s, low], ph, RAW_A, zm).start()

    def slot_of(ph, k):
        return 2 * ORDER.index((ph, k)) + 1

    def forward(ph):
        s_next, s_prev = slot_of(ph, 1), slot_of(ph, 3)
        ring_copy(part.at[s_next, low], ph, R1, zp).wait_recv()
        part[s_next, :RANK, :] = part[s_next, :RANK, :] + rsr[ph * 6 + R1]
        ring_copy(part.at[s_next, low], ph, COMB_A, zp).start()
        ring_copy(part.at[s_prev, high], ph, R2, zm).wait_recv()
        part[s_prev, RANK:, :] = part[s_prev, RANK:, :] + rsr[ph * 6 + R2]
        ring_copy(part.at[s_prev, high], ph, COMB_B, zm).start()

    def finish(ph):
        s = slot_of(ph, 0)
        for slot in (RAW_A, RAW_B, COMB_A, COMB_B):
            ring_copy(part.at[s, low], ph, slot, zp).wait_recv()
        top = part[s, :RANK, :] + rsr[ph * 6 + RAW_A] + rsr[ph * 6 + COMB_A]
        bottom = part[s, RANK:, :] + rsr[ph * 6 + RAW_B] + rsr[ph * 6 + COMB_B]
        return gradient(top, bottom)

    w_copies[0].wait()
    project_out(0)
    project_out(1)
    for s in range(2, AHEAD):
        start_item(s)
    pl.semaphore_wait(bar, NM - 1 + 6)
    sib_half(low, 0).start()
    for o in range(1, 4):
        pl.semaphore_signal(xsem, inc=1, device_id=(y * NX + (x + o) % NX, mp), device_id_type=MESH)
    w_copies[1].wait()
    project_in(0)
    sib_half(high, PAIRS).start()
    project_in(1)
    for s in range(AHEAD, AHEAD + 2):
        start_item(s)
    sib_half(low, 0).wait_recv()
    part[1, :RANK, :] = part[1, :RANK, :] + sibr[0, :RANK, :]
    ring_copy(part.at[1, low], 0, R1, zp).start()

    def pair(q, carry):
        project_pair(q)
        sib_copy(q).start()
        start_item(2 * q + AHEAD)
        start_item(2 * q + 1 + AHEAD)
        @pl.when(q == 1)
        def _():
            sib_half(high, PAIRS).wait_recv()
            part[1, RANK:, :] = part[1, RANK:, :] + sibr[0, RANK:, :]
            ring_copy(part.at[1, high], 0, R2, zm).start()

        @pl.when(q > LAG)
        def _():
            merge(q - LAG)

        @pl.when(q == FORWARD_AT)
        def _():
            forward(0)

        return carry

    lax.fori_loop(1, PAIRS, pair, 0)
    for q in range(PAIRS - LAG, PAIRS):
        merge(q)
    forward(1)

    own_d, own_m = pl.ds(pl.multiple_of(dp * ROWS, ROWS), ROWS), pl.ds(pl.multiple_of(mp * ROWS, ROWS), ROWS)

    def mp_copy(o, src, dst, ss, rs):
        return pltpu.make_async_remote_copy(
            src_ref=src, dst_ref=dst.at[own_m], send_sem=ss, recv_sem=rs, device_id=(dp, (mp + o) % NM), device_id_type=MESH
        )

    def dp_copy(o, src, dst, ss, rs):
        return pltpu.make_async_remote_copy(
            src_ref=src, dst_ref=dst.at[own_d], send_sem=ss, recv_sem=rs, device_id=((dp + o) % ND, mp), device_id_type=MESH
        )

    train_row = finish(0)
    t_own[...] = train_row
    pl.semaphore_wait(xsem, 3)
    for o in range(1, ND):
        dp_copy(o, t_own, t_m, t_ss.at[0], t_rs.at[0]).start()
    for o in range(1, NM):
        mp_copy(o, t_own, t_g, t_ss.at[1], t_rs.at[1]).start()
    t_m[own_d, :] = train_row
    t_g[own_m, :] = train_row

    target_row = finish(1)
    b_own[...] = target_row
    for o in range(1, NM):
        mp_copy(o, b_own, b_g, b_ss, b_rs).start()
    b_g[own_m, :] = target_row
    b_norm = jnp.sum(target_row * target_row)

    def bytes_of(ref, sem):
        return pltpu.make_async_copy(ref, ref, sem)

    dp_rest, mp_rest = pl.ds(0, (ND - 1) * ROWS), pl.ds(0, (NM - 1) * ROWS)
    bytes_of(t_m.at[dp_rest], t_rs.at[0]).wait()
    bytes_of(t_g.at[mp_rest], t_rs.at[1]).wait()
    place = ((mp + 1) % NM) * ND + dp
    msg[1:2, :] = jnp.where(iota((1, LANES), 1) == place, b_norm, block_row(t_g, t_m))
    bytes_of(b_g.at[mp_rest], b_rs).wait()
    msg[0:1, :] = block_row(b_g, t_m)

    me = dp * NM + mp

    to_dps = [((y + dy) % 4) * NX + (x + dx) % NX for dy in (2, 1, 3, 0) for dx in (2, 1, 3, 0)]
    to_mps = [((z + dz) % NZ) * 2 + (c + dc) % 2 for dz in (2, 1, 3, 0) for dc in (1, 0)]
    for to in [(to_dp, to_mp) for to_dp in to_dps for to_mp in to_mps][:-1]:
        pltpu.make_async_remote_copy(
            src_ref=msg, dst_ref=fin.at[me], send_sem=f_ss, recv_sem=f_rs, device_id=to, device_id_type=MESH
        ).start()
    fin[me] = msg[...]
    bytes_of(fin.at[pl.ds(0, NDEV - 1)], f_rs).wait()

    for d in range(ND):
        rows = pl.ds(d * NM, NM)
        c_mat[rows, :] = swap_blocks(fin[rows, 0, :])
        k_mat[pl.ds(d, NM, stride=ND), :] = swap_blocks(fin[rows, 1, :])
    lane, sub = iota((NDEV, LANES), 1), iota((NDEV, LANES), 0)
    sent = k_mat[...]
    taken = sub == (lane + ND) % LANES
    norm_row = jnp.sum(jnp.where(taken, sent, 0.0), axis=0, keepdims=True)
    norm = jnp.sum(jnp.where(lane == (sub % NM) * ND + sub // NM, norm_row, 0.0), axis=1, keepdims=True)
    mirror = jnp.sum(jnp.where(lane == sub, pltpu.roll(sent, LANES - ND, 1), 0.0), axis=0, keepdims=True)
    gram = jnp.where(taken, mirror, sent)
    trace = jnp.sum(jnp.where(lane == sub, gram, 0.0), keepdims=True)
    damping = trace * (0.1 / (NDEV * RANK * RANK))
    inv = 1.0 / NDEV
    u_res = c_mat[...]
    u_dir, scores, dir_norm = u_res, jnp.zeros_like(u_res), norm
    for step in range(ITERS):
        u_norm = jnp.sum(u_dir * u_dir, axis=1, keepdims=True)
        alpha = norm / (damping * dir_norm + u_norm * inv)
        scores = scores + alpha * u_dir
        if step == ITERS - 1:
            break
        image = lax.dot_general(u_dir, gram, (((1,), (0,)), ((), ())), precision=lax.Precision.HIGHEST, preferred_element_type=F32)
        u_gram = jnp.sum(u_dir * image, axis=1, keepdims=True)
        squared = damping * damping * dir_norm + 2.0 * inv * damping * u_norm + inv * inv * u_gram
        following = alpha * alpha * squared - norm
        u_res = u_res - alpha * (damping * u_dir + inv * image)
        ratio = following / norm
        u_dir = u_res + ratio * u_dir
        dir_norm = following + ratio * ratio * dir_norm
        norm = following
    column = jnp.sum(jnp.where(lane == mp * ND + dp, scores, 0.0), axis=1, keepdims=True)
    spread = jnp.where(lane == sub, column, 0.0)
    out_ref[...] = sum(spread[8 * d : 8 * d + 8, :] for d in range(ND))

    bytes_of(part.at[pl.ds(0, PAIRS)], sib_ss).wait()
    bytes_of(rsr, rs_ss).wait()
    bytes_of(t_m.at[dp_rest], t_ss.at[0]).wait()
    bytes_of(t_g.at[mp_rest], t_ss.at[1]).wait()
    bytes_of(b_g.at[mp_rest], b_ss).wait()
    bytes_of(fin.at[pl.ds(0, NDEV - 1)], f_ss).wait()


def local(train_in, train_grad_out, target_in, target_grad_out, proj_in, proj_out):
    d_in, d_out = proj_in.shape[1], proj_out.shape[1]
    dma, vmem = pltpu.SemaphoreType.DMA, pltpu.VMEM
    spread = pl.pallas_call(
        kernel,
        out_shape=jax.ShapeDtypeStruct((8, NDEV), F32),
        in_specs=[pl.BlockSpec(memory_space=pltpu.HBM)] * 6,
        out_specs=pl.BlockSpec(memory_space=pltpu.VMEM),
        scratch_shapes=[
            vmem((2 * PAIRS, d_in, SEQ), BF16),
            vmem((2 * PAIRS, SEQ, d_out), BF16),
            vmem((RANK, d_in), BF16),
            vmem((RANK, d_out), BF16),
            vmem((2 * PAIRS, 2 * RANK, SEQ), F32),
            vmem((PAIRS, 2 * RANK, SEQ), F32),
            vmem((12, RANK, SEQ), F32),
            vmem((ROWS, LANES), F32),
            vmem((ROWS, LANES), F32),
            vmem((ND * ROWS, LANES), F32),
            vmem((NM * ROWS, LANES), F32),
            vmem((NM * ROWS, LANES), F32),
            vmem((2, LANES), F32),
            vmem((NDEV, 2, LANES), F32),
            vmem((NDEV, LANES), F32),
            vmem((NDEV, LANES), F32),
            dma((2 * PAIRS, 2)),
            dma((2,)),
            dma,
            dma((PAIRS + 1,)),
            dma,
            dma((12,)),
            dma((2,)),
            dma((2,)),
            dma,
            dma,
            dma,
            dma,
            pltpu.SemaphoreType.REGULAR,
        ],
        compiler_params=pltpu.CompilerParams(collective_id=0, has_side_effects=True, vmem_limit_bytes=32 * 1024 * 1024),
    )(*(
        pltpu.with_memory_space_constraint(a, pltpu.HBM)
        for a in (train_in.swapaxes(1, 2), train_grad_out, target_in.swapaxes(1, 2), target_grad_out, proj_in, proj_out)
    ))
    return jnp.sum(spread, axis=0, keepdims=True)


def solution(mesh):
    return jax.shard_map(
        local,
        mesh=mesh,
        in_specs=(
            P("dp", None, "mp"),
            P("dp", None, "mp"),
            P("dp", None, "mp"),
            P("dp", None, "mp"),
            P(None, "mp"),
            P(None, "mp"),
        ),
        out_specs=P(("dp", "mp"), None),
        check_vma=False,
    )
```

```python
import functools

import jax
import jax.numpy as jnp
from jax import lax
from jax.experimental import pallas as pl
from jax.experimental.pallas import tpu as pltpu
from jax.sharding import PartitionSpec as P

MESH = pl.DeviceIdType.MESH
F32 = jnp.float32
BF16 = jnp.bfloat16
ITERS = 4
ND, NM, NX, NZ = 16, 8, 4, 4
NDEV = ND * NM
SEQ, LANES, RANK = 256, 128, 64
ROWS = RANK * RANK // LANES
PAIRS = 8
AHEAD = 6
LAG = 2
SPLIT = 2
FORWARD_AT = 6
ORDER = ((0, 2), (1, 2), (0, 1), (0, 3), (1, 1), (1, 3), (0, 0), (1, 0))
PHASE_BITS = sum(ph << q for q, (ph, _) in enumerate(ORDER))
CHIP_BITS = sum(k << 2 * q for q, (_, k) in enumerate(ORDER))
R1, R2, RAW_A, RAW_B, COMB_A, COMB_B = range(6)


def iota(shape, axis):
    return lax.broadcasted_iota(jnp.int32, shape, axis)


def thirds(value):
    first = value.astype(BF16)
    left = value - first.astype(F32)
    second = left.astype(BF16)
    return first, second, (left - second.astype(F32)).astype(BF16)


def block_row(rows_ref, tile_ref):
    def body(k, acc):
        tiles = [tile_ref[pl.ds(t * 8 * ROWS + k, 8, stride=ROWS), :] for t in range(2)]
        new = []
        for e in range(NM):
            row = rows_ref[pl.ds(e * ROWS + k, 1), :]
            for t in range(2):
                new.append(acc[e * 2 + t] + tiles[t] * row)
        return tuple(new)

    acc = lax.fori_loop(0, ROWS, body, tuple(jnp.zeros((8, LANES), F32) for _ in range(2 * NM)), unroll=4)
    lane, sub = iota((8, LANES), 1), iota((8, LANES), 0)
    spread = jnp.zeros((8, LANES), F32)
    for i in range(2 * NM):
        spread = jnp.where(lane // 8 == i, jnp.sum(acc[i], axis=1, keepdims=True), spread)
    return jnp.sum(jnp.where(lane % 8 == sub, spread, 0.0), axis=0, keepdims=True)


def swap_blocks(tile):
    diag = iota((8, LANES), 1) // 16 == iota((8, LANES), 0)
    out = jnp.where(diag, tile, 0.0)
    for s in range(1, 8):
        moved = jnp.where(diag, pltpu.roll(tile, s * 16, 1), 0.0)
        out = out + pltpu.roll(moved, 8 - s, 0)
    return out


def gradient(out_part, in_part):
    outer = lax.dot_general(
        out_part, in_part, (((1,), (1,)), ((), ())), precision=lax.Precision.HIGHEST, preferred_element_type=F32
    )
    return jnp.concatenate([outer[: RANK // 2, :], outer[RANK // 2 :, :]], axis=1) * (1.0 / SEQ)


def kernel(
    train_in, train_go, target_in, target_go, proj_in, proj_out, out_ref,
    xin, xgo, w_in, w_out, part, sibr, rsr, t_own, b_own, t_m, t_g, b_g, msg, fin, c_mat, k_mat,
    in_sem, w_sem, sib_ss, sib_rs, rs_ss, rs_rs, t_ss, t_rs, b_ss, b_rs, f_ss, f_rs, xsem,
):
    dp, mp = lax.axis_index("dp"), lax.axis_index("mp")
    y, x, z, c = dp // NX, dp % NX, mp // 2, mp % 2
    zp, zm = ((z + 1) % NZ) * 2 + c, ((z + 3) % NZ) * 2 + c

    def item_copies(s, source_in, source_go):
        k = lax.shift_right_logical(CHIP_BITS, 2 * (s // 2)) & 3
        e = ((z + k) % NZ) * 2 + (c + 1 + s) % 2
        return (
            pltpu.make_async_copy(source_in.at[e], xin.at[s], in_sem.at[s, 0]),
            pltpu.make_async_copy(source_go.at[e], xgo.at[s], in_sem.at[s, 1]),
        )

    def start_item(s):
        phase = lax.shift_right_logical(PHASE_BITS, s // 2) & 1

        @pl.when((phase == 0) & (s < 2 * PAIRS))
        def _():
            for copy in item_copies(s, train_in, train_go):
                copy.start()

        @pl.when((phase == 1) & (s < 2 * PAIRS))
        def _():
            for copy in item_copies(s, target_in, target_go):
                copy.start()

    w_copies = (pltpu.make_async_copy(proj_out, w_out, w_sem.at[0]), pltpu.make_async_copy(proj_in, w_in, w_sem.at[1]))
    sources = ((train_in, train_go), (target_in, target_go))
    first = [item_copies(s, *sources[ORDER[s // 2][0]]) for s in range(2 * SPLIT)]
    w_copies[0].start()
    for copies in first:
        copies[1].start()
    w_copies[1].start()
    for copies in first[:2]:
        copies[0].start()

    bar = pltpu.get_barrier_semaphore()
    for o in range(1, NM):
        pl.semaphore_signal(bar, inc=1, device_id=(dp, (mp + o) % NM), device_id_type=MESH)
    for o in range(1, 4):
        pl.semaphore_signal(bar, inc=1, device_id=(y * NX + (x + o) % NX, mp), device_id_type=MESH)
        pl.semaphore_signal(bar, inc=1, device_id=(((y + o) % 4) * NX + x, mp), device_id_type=MESH)

    def project_out(items):
        for s in items:
            item_copies(s, train_in, train_go)[1].wait()
        for s in items:
            part[s, :RANK, :] = lax.dot_general(w_out[...], xgo[s], (((1,), (1,)), ((), ())), preferred_element_type=F32)

    def project_in(items):
        for s in items:
            item_copies(s, train_in, train_go)[0].wait()
        for s in items:
            part[s, RANK:, :] = jnp.dot(w_in[...], xin[s], preferred_element_type=F32)

    low, high = pl.ds(0, RANK), pl.ds(RANK, RANK)

    def sib_half(q, half, sem):
        return pltpu.make_async_remote_copy(
            src_ref=part.at[2 * q, half], dst_ref=sibr.at[q, half], send_sem=sib_ss, recv_sem=sib_rs.at[sem],
            device_id=(dp, z * 2 + (1 - c)), device_id_type=MESH,
        )

    def project_pair(q):
        for s in (2 * q, 2 * q + 1):
            for copy in item_copies(s, train_in, train_go):
                copy.wait()
        for s in (2 * q, 2 * q + 1):
            part[s, :RANK, :] = lax.dot_general(w_out[...], xgo[s], (((1,), (1,)), ((), ())), preferred_element_type=F32)
            part[s, RANK:, :] = jnp.dot(w_in[...], xin[s], preferred_element_type=F32)

    def sib_copy(q):
        return pltpu.make_async_remote_copy(
            src_ref=part.at[2 * q], dst_ref=sibr.at[q], send_sem=sib_ss, recv_sem=sib_rs.at[q],
            device_id=(dp, z * 2 + (1 - c)), device_id_type=MESH,
        )

    def ring_copy(src, ph, slot, to):
        return pltpu.make_async_remote_copy(
            src_ref=src, dst_ref=rsr.at[ph * 6 + slot], send_sem=rs_ss, recv_sem=rs_rs.at[ph * 6 + slot],
            device_id=(dp, to), device_id_type=MESH,
        )

    def merge(q):
        sib_copy(q).wait_recv()
        s = 2 * q + 1
        part[s] = part[s] + sibr[q]
        for j, (ph, k) in list(enumerate(ORDER))[SPLIT:]:

            @pl.when(q == j)
            def _():
                if k == 2:
                    ring_copy(part.at[s, low], ph, R1, zp).start()
                    ring_copy(part.at[s, high], ph, R2, zm).start()
                if k == 1:
                    ring_copy(part.at[s, high], ph, RAW_B, zp).start()
                if k == 3:
                    ring_copy(part.at[s, low], ph, RAW_A, zm).start()

    def slot_of(ph, k):
        return 2 * ORDER.index((ph, k)) + 1

    def forward(ph):
        s_next, s_prev = slot_of(ph, 1), slot_of(ph, 3)
        ring_copy(part.at[s_next, low], ph, R1, zp).wait_recv()
        part[s_next, :RANK, :] = part[s_next, :RANK, :] + rsr[ph * 6 + R1]
        ring_copy(part.at[s_next, low], ph, COMB_A, zp).start()
        ring_copy(part.at[s_prev, high], ph, R2, zm).wait_recv()
        part[s_prev, RANK:, :] = part[s_prev, RANK:, :] + rsr[ph * 6 + R2]
        ring_copy(part.at[s_prev, high], ph, COMB_B, zm).start()

    def finish(ph):
        s = slot_of(ph, 0)
        for slot in (RAW_A, RAW_B, COMB_A, COMB_B):
            ring_copy(part.at[s, low], ph, slot, zp).wait_recv()
        top = part[s, :RANK, :] + rsr[ph * 6 + RAW_A] + rsr[ph * 6 + COMB_A]
        bottom = part[s, RANK:, :] + rsr[ph * 6 + RAW_B] + rsr[ph * 6 + COMB_B]
        return gradient(top, bottom)

    w_copies[0].wait()
    project_out(range(2 * SPLIT))
    for copies in first[2:]:
        copies[0].start()
    for s in range(2 * SPLIT, AHEAD):
        start_item(s)
    pl.semaphore_wait(bar, NM - 1 + 6)
    for q in range(SPLIT):
        sib_half(q, low, q).start()
    for o in range(1, 4):
        pl.semaphore_signal(xsem, inc=1, device_id=(y * NX + (x + o) % NX, mp), device_id_type=MESH)
    w_copies[1].wait()
    for q in range(SPLIT):
        project_in((2 * q, 2 * q + 1))
        sib_half(q, high, PAIRS + q).start()
        for s in range(2 * q + AHEAD, 2 * q + 2 + AHEAD):
            start_item(s)
        if q == 0:
            for p in range(SPLIT):
                sib_half(p, low, p).wait_recv()
                part[2 * p + 1, :RANK, :] = part[2 * p + 1, :RANK, :] + sibr[p, :RANK, :]
                ring_copy(part.at[2 * p + 1, low], ORDER[p][0], R1, zp).start()

    def merge_high(p):
        sib_half(p, high, PAIRS + p).wait_recv()
        part[2 * p + 1, RANK:, :] = part[2 * p + 1, RANK:, :] + sibr[p, RANK:, :]
        ring_copy(part.at[2 * p + 1, high], ORDER[p][0], R2, zm).start()

    merge_high(0)

    def pair(q, carry):
        project_pair(q)
        sib_copy(q).start()
        start_item(2 * q + AHEAD)
        start_item(2 * q + 1 + AHEAD)
        @pl.when(q == SPLIT)
        def _():
            merge_high(1)

        @pl.when(q >= SPLIT + LAG)
        def _():
            merge(q - LAG)

        @pl.when(q == FORWARD_AT)
        def _():
            forward(0)

        return carry

    lax.fori_loop(SPLIT, PAIRS, pair, 0)
    for q in range(PAIRS - LAG, PAIRS):
        merge(q)
    forward(1)

    own_d, own_m = pl.ds(pl.multiple_of(dp * ROWS, ROWS), ROWS), pl.ds(pl.multiple_of(mp * ROWS, ROWS), ROWS)

    def mp_copy(o, src, dst, ss, rs):
        return pltpu.make_async_remote_copy(
            src_ref=src, dst_ref=dst.at[own_m], send_sem=ss, recv_sem=rs, device_id=(dp, (mp + o) % NM), device_id_type=MESH
        )

    def to_sibling(src, rows):
        return pltpu.make_async_remote_copy(
            src_ref=src, dst_ref=t_g.at[rows], send_sem=t_ss.at[1], recv_sem=t_rs.at[2],
            device_id=(dp, z * 2 + (1 - c)), device_id_type=MESH,
        )

    def dp_copy(o, src, dst, ss, rs):
        return pltpu.make_async_remote_copy(
            src_ref=src, dst_ref=dst.at[own_d], send_sem=ss, recv_sem=rs, device_id=((dp + o) % ND, mp), device_id_type=MESH
        )

    train_row = finish(0)
    t_own[...] = train_row
    pl.semaphore_wait(xsem, 3)
    for o in range(1, ND):
        dp_copy(o, t_own, t_m, t_ss.at[0], t_rs.at[0]).start()
    for dz in range(1, NZ):
        mp_copy(2 * dz, t_own, t_g, t_ss.at[1], t_rs.at[1]).start()
    to_sibling(t_own, own_m).start()
    t_m[own_d, :] = train_row
    t_g[own_m, :] = train_row

    target_row = finish(1)
    b_own[...] = target_row
    for o in range(1, NM):
        mp_copy(o, b_own, b_g, b_ss, b_rs).start()
    b_g[own_m, :] = target_row
    b_norm = jnp.sum(target_row * target_row)

    def bytes_of(ref, sem):
        return pltpu.make_async_copy(ref, ref, sem)

    dp_rest, mp_rest = pl.ds(0, (ND - 1) * ROWS), pl.ds(0, (NM - 1) * ROWS)
    bytes_of(t_g.at[pl.ds(0, (NZ - 1) * ROWS)], t_rs.at[1]).wait()
    for dz in range(1, NZ):
        rows = pl.ds(pl.multiple_of((((z + dz) % NZ) * 2 + c) * ROWS, ROWS), ROWS)
        to_sibling(t_g.at[rows], rows).start()
    bytes_of(t_m.at[dp_rest], t_rs.at[0]).wait()
    bytes_of(t_g.at[pl.ds(0, NZ * ROWS)], t_rs.at[2]).wait()
    place = ((mp + 1) % NM) * ND + dp
    msg[1:2, :] = jnp.where(iota((1, LANES), 1) == place, b_norm, block_row(t_g, t_m))
    bytes_of(b_g.at[mp_rest], b_rs).wait()
    msg[0:1, :] = block_row(b_g, t_m)

    me = dp * NM + mp

    to_dps = [((y + dy) % 4) * NX + (x + dx) % NX for dy in (2, 1, 3, 0) for dx in (2, 1, 3, 0)]
    to_mps = [((z + dz) % NZ) * 2 + (c + dc) % 2 for dz in (2, 1, 3, 0) for dc in (1, 0)]
    for to in [(to_dp, to_mp) for to_mp in to_mps for to_dp in to_dps][:-1]:
        pltpu.make_async_remote_copy(
            src_ref=msg, dst_ref=fin.at[me], send_sem=f_ss, recv_sem=f_rs, device_id=to, device_id_type=MESH
        ).start()
    fin[me] = msg[...]
    bytes_of(fin.at[pl.ds(0, NDEV - 1)], f_rs).wait()

    for d in range(ND):
        rows, spaced = pl.ds(d * NM, NM), pl.ds(d, NM, stride=ND)
        c_mat[spaced, :] = swap_blocks(fin[rows, 0, :])
        k_mat[spaced, :] = swap_blocks(fin[rows, 1, :])
    lane, sub = iota((NDEV, LANES), 1), iota((NDEV, LANES), 0)
    sent = k_mat[...]
    taken = sub == (lane + ND) % LANES
    norm = jnp.sum(jnp.where(taken, sent, 0.0), axis=0, keepdims=True)
    mirror = jnp.sum(jnp.where(lane == sub, pltpu.roll(sent, LANES - ND, 1), 0.0), axis=0, keepdims=True)
    gram = jnp.where(taken, mirror, sent)
    trace = jnp.sum(jnp.where(lane == sub, gram, 0.0), axis=0, keepdims=True)
    damping = jnp.sum(trace, axis=1, keepdims=True) * (0.1 / (NDEV * RANK * RANK))
    inv = 1.0 / NDEV
    g_first, g_second, g_third = thirds(gram)
    gram_leading = jnp.concatenate(
        [jnp.concatenate([g_first, g_first], axis=1), jnp.concatenate([g_second, g_second], axis=1)], axis=0
    )
    gram_rest = jnp.concatenate([g_third, g_first], axis=1)
    u_res = c_mat[...].T
    u_dir, scores, dir_norm = u_res, jnp.zeros_like(u_res), norm
    for step in range(ITERS):
        u_norm = jnp.sum(u_dir * u_dir, axis=0, keepdims=True)
        alpha = norm / (damping * dir_norm + u_norm * inv)
        scores = scores + alpha * u_dir
        if step == ITERS - 1:
            break
        u_first, u_second, u_third = thirds(u_dir)
        leading = jnp.dot(gram_leading, jnp.concatenate([u_first, u_second], axis=0), preferred_element_type=F32)
        rest = jnp.dot(gram_rest, jnp.concatenate([u_first, u_third], axis=0), preferred_element_type=F32)
        image = (rest + leading[NDEV:, :]) + leading[:NDEV, :]
        u_gram = jnp.sum(u_dir * image, axis=0, keepdims=True)
        squared = damping * damping * dir_norm + 2.0 * inv * damping * u_norm + inv * inv * u_gram
        following = alpha * alpha * squared - norm
        u_res = u_res - alpha * (damping * u_dir + inv * image)
        ratio = following / norm
        u_dir = u_res + ratio * u_dir
        dir_norm = following + ratio * ratio * dir_norm
        norm = following
    row = jnp.sum(jnp.where(sub == mp * ND + dp, scores, 0.0), axis=0, keepdims=True)
    column = jnp.sum(jnp.where(lane == sub, row, 0.0), axis=1, keepdims=True)
    spread = jnp.where(lane == (sub % ND) * NM + sub // ND, column, 0.0)
    out_ref[...] = sum(spread[8 * d : 8 * d + 8, :] for d in range(ND))

    bytes_of(part.at[pl.ds(0, PAIRS)], sib_ss).wait()
    bytes_of(rsr, rs_ss).wait()
    bytes_of(t_m.at[dp_rest], t_ss.at[0]).wait()
    bytes_of(t_g.at[mp_rest], t_ss.at[1]).wait()
    bytes_of(b_g.at[mp_rest], b_ss).wait()
    bytes_of(fin.at[pl.ds(0, NDEV - 1)], f_ss).wait()


def local(train_in, train_grad_out, target_in, target_grad_out, proj_in, proj_out):
    d_in, d_out = proj_in.shape[1], proj_out.shape[1]
    dma, vmem = pltpu.SemaphoreType.DMA, pltpu.VMEM
    spread = pl.pallas_call(
        kernel,
        out_shape=jax.ShapeDtypeStruct((8, NDEV), F32),
        in_specs=[pl.BlockSpec(memory_space=pltpu.HBM)] * 6,
        out_specs=pl.BlockSpec(memory_space=pltpu.VMEM),
        scratch_shapes=[
            vmem((2 * PAIRS, d_in, SEQ), BF16),
            vmem((2 * PAIRS, SEQ, d_out), BF16),
            vmem((RANK, d_in), BF16),
            vmem((RANK, d_out), BF16),
            vmem((2 * PAIRS, 2 * RANK, SEQ), F32),
            vmem((PAIRS, 2 * RANK, SEQ), F32),
            vmem((12, RANK, SEQ), F32),
            vmem((ROWS, LANES), F32),
            vmem((ROWS, LANES), F32),
            vmem((ND * ROWS, LANES), F32),
            vmem((NM * ROWS, LANES), F32),
            vmem((NM * ROWS, LANES), F32),
            vmem((2, LANES), F32),
            vmem((NDEV, 2, LANES), F32),
            vmem((NDEV, LANES), F32),
            vmem((NDEV, LANES), F32),
            dma((2 * PAIRS, 2)),
            dma((2,)),
            dma,
            dma((PAIRS + SPLIT,)),
            dma,
            dma((12,)),
            dma((2,)),
            dma((3,)),
            dma,
            dma,
            dma,
            dma,
            pltpu.SemaphoreType.REGULAR,
        ],
        compiler_params=pltpu.CompilerParams(collective_id=0, has_side_effects=True, vmem_limit_bytes=32 * 1024 * 1024),
    )(*(
        pltpu.with_memory_space_constraint(a, pltpu.HBM)
        for a in (train_in.swapaxes(1, 2), train_grad_out, target_in.swapaxes(1, 2), target_grad_out, proj_in, proj_out)
    ))
    return jnp.sum(spread, axis=0, keepdims=True)


def solution(mesh):
    return jax.shard_map(
        local,
        mesh=mesh,
        in_specs=(
            P("dp", None, "mp"),
            P("dp", None, "mp"),
            P("dp", None, "mp"),
            P("dp", None, "mp"),
            P(None, "mp"),
            P(None, "mp"),
        ),
        out_specs=P(("dp", "mp"), None),
        check_vma=False,
    )
```

```python
import functools

import jax
import jax.numpy as jnp
from jax import lax
from jax.experimental import pallas as pl
from jax.experimental.pallas import tpu as pltpu
from jax.sharding import PartitionSpec as P

MESH = pl.DeviceIdType.MESH
F32 = jnp.float32
BF16 = jnp.bfloat16
ITERS = 4
ND, NM, NX, NZ = 16, 8, 4, 4
NDEV = ND * NM
SEQ, LANES, RANK = 256, 128, 64
ROWS = RANK * RANK // LANES
PAIRS = 8
AHEAD = 6
LAG = 2
SPLIT = 2
FORWARD_AT = 6
ORDER = ((0, 2), (1, 2), (0, 1), (0, 3), (1, 1), (1, 3), (0, 0), (1, 0))
PHASE_BITS = sum(ph << q for q, (ph, _) in enumerate(ORDER))
CHIP_BITS = sum(k << 2 * q for q, (_, k) in enumerate(ORDER))
R1, R2, RAW_A, RAW_B, COMB_A, COMB_B = range(6)


def iota(shape, axis):
    return lax.broadcasted_iota(jnp.int32, shape, axis)


def thirds(value):
    first = value.astype(BF16)
    left = value - first.astype(F32)
    second = left.astype(BF16)
    return first, second, (left - second.astype(F32)).astype(BF16)


def block_row(rows_ref, tile_ref):
    def body(k, acc):
        tiles = [tile_ref[pl.ds(t * 8 * ROWS + k, 8, stride=ROWS), :] for t in range(2)]
        new = []
        for e in range(NM):
            row = rows_ref[pl.ds(e * ROWS + k, 1), :]
            for t in range(2):
                new.append(acc[e * 2 + t] + tiles[t] * row)
        return tuple(new)

    acc = lax.fori_loop(0, ROWS, body, tuple(jnp.zeros((8, LANES), F32) for _ in range(2 * NM)), unroll=8)
    lane, sub = iota((8, LANES), 1), iota((8, LANES), 0)
    spread = jnp.zeros((8, LANES), F32)
    for i in range(2 * NM):
        spread = jnp.where(lane // 8 == i, jnp.sum(acc[i], axis=1, keepdims=True), spread)
    return jnp.sum(jnp.where(lane % 8 == sub, spread, 0.0), axis=0, keepdims=True)


def swap_blocks(tile):
    diag = iota((8, LANES), 1) // 16 == iota((8, LANES), 0)
    out = jnp.where(diag, tile, 0.0)
    for s in range(1, 8):
        moved = jnp.where(diag, pltpu.roll(tile, s * 16, 1), 0.0)
        out = out + pltpu.roll(moved, 8 - s, 0)
    return out


def gradient(out_part, in_part):
    outer = lax.dot_general(
        out_part, in_part, (((1,), (1,)), ((), ())), precision=lax.Precision.HIGHEST, preferred_element_type=F32
    )
    return jnp.concatenate([outer[: RANK // 2, :], outer[RANK // 2 :, :]], axis=1) * (1.0 / SEQ)


def kernel(
    train_in, train_go, target_in, target_go, proj_in, proj_out, out_ref,
    xin, xgo, w_in, w_out, part, sibr, rsr, t_own, b_own, t_m, t_g, b_g, msg, fin, c_mat, k_mat,
    in_sem, w_sem, sib_ss, sib_rs, rs_ss, rs_rs, t_ss, t_rs, b_ss, b_rs, f_ss, f_rs, xsem,
):
    dp, mp = lax.axis_index("dp"), lax.axis_index("mp")
    y, x, z, c = dp // NX, dp % NX, mp // 2, mp % 2
    zp, zm = ((z + 1) % NZ) * 2 + c, ((z + 3) % NZ) * 2 + c

    def item_copies(s, source_in, source_go):
        k = lax.shift_right_logical(CHIP_BITS, 2 * (s // 2)) & 3
        e = ((z + k) % NZ) * 2 + (c + 1 + s) % 2
        return (
            pltpu.make_async_copy(source_in.at[e], xin.at[s], in_sem.at[s, 0]),
            pltpu.make_async_copy(source_go.at[e], xgo.at[s], in_sem.at[s, 1]),
        )

    def start_item(s):
        phase = lax.shift_right_logical(PHASE_BITS, s // 2) & 1

        @pl.when((phase == 0) & (s < 2 * PAIRS))
        def _():
            for copy in item_copies(s, train_in, train_go):
                copy.start()

        @pl.when((phase == 1) & (s < 2 * PAIRS))
        def _():
            for copy in item_copies(s, target_in, target_go):
                copy.start()

    w_copies = (pltpu.make_async_copy(proj_out, w_out, w_sem.at[0]), pltpu.make_async_copy(proj_in, w_in, w_sem.at[1]))
    sources = ((train_in, train_go), (target_in, target_go))
    first = [item_copies(s, *sources[ORDER[s // 2][0]]) for s in range(2 * SPLIT)]
    w_copies[0].start()
    for copies in first:
        copies[1].start()
    w_copies[1].start()
    for copies in first[:2]:
        copies[0].start()

    bar = pltpu.get_barrier_semaphore()
    for o in range(1, NM):
        pl.semaphore_signal(bar, inc=1, device_id=(dp, (mp + o) % NM), device_id_type=MESH)
    for o in range(1, 4):
        pl.semaphore_signal(bar, inc=1, device_id=(y * NX + (x + o) % NX, mp), device_id_type=MESH)
        pl.semaphore_signal(bar, inc=1, device_id=(((y + o) % 4) * NX + x, mp), device_id_type=MESH)

    def project_out(items):
        for s in items:
            item_copies(s, train_in, train_go)[1].wait()
        for s in items:
            part[s, :RANK, :] = lax.dot_general(w_out[...], xgo[s], (((1,), (1,)), ((), ())), preferred_element_type=F32)

    def project_in(items):
        for s in items:
            item_copies(s, train_in, train_go)[0].wait()
        for s in items:
            part[s, RANK:, :] = jnp.dot(w_in[...], xin[s], preferred_element_type=F32)

    low, high = pl.ds(0, RANK), pl.ds(RANK, RANK)

    def sib_half(q, half, sem):
        return pltpu.make_async_remote_copy(
            src_ref=part.at[2 * q, half], dst_ref=sibr.at[q, half], send_sem=sib_ss, recv_sem=sib_rs.at[sem],
            device_id=(dp, z * 2 + (1 - c)), device_id_type=MESH,
        )

    def project_pair(q):
        for s in (2 * q, 2 * q + 1):
            for copy in item_copies(s, train_in, train_go):
                copy.wait()
        for s in (2 * q, 2 * q + 1):
            part[s, :RANK, :] = lax.dot_general(w_out[...], xgo[s], (((1,), (1,)), ((), ())), preferred_element_type=F32)
            part[s, RANK:, :] = jnp.dot(w_in[...], xin[s], preferred_element_type=F32)

    def sib_copy(q):
        return pltpu.make_async_remote_copy(
            src_ref=part.at[2 * q], dst_ref=sibr.at[q], send_sem=sib_ss, recv_sem=sib_rs.at[q],
            device_id=(dp, z * 2 + (1 - c)), device_id_type=MESH,
        )

    def ring_copy(src, ph, slot, to):
        return pltpu.make_async_remote_copy(
            src_ref=src, dst_ref=rsr.at[ph * 6 + slot], send_sem=rs_ss, recv_sem=rs_rs.at[ph * 6 + slot],
            device_id=(dp, to), device_id_type=MESH,
        )

    def merge(q):
        sib_copy(q).wait_recv()
        s = 2 * q + 1
        part[s] = part[s] + sibr[q]
        for j, (ph, k) in list(enumerate(ORDER))[SPLIT:]:

            @pl.when(q == j)
            def _():
                if k == 2:
                    ring_copy(part.at[s, low], ph, R1, zp).start()
                    ring_copy(part.at[s, high], ph, R2, zm).start()
                if k == 1:
                    ring_copy(part.at[s, high], ph, RAW_B, zp).start()
                if k == 3:
                    ring_copy(part.at[s, low], ph, RAW_A, zm).start()

    def slot_of(ph, k):
        return 2 * ORDER.index((ph, k)) + 1

    def forward(ph):
        s_next, s_prev = slot_of(ph, 1), slot_of(ph, 3)
        ring_copy(part.at[s_next, low], ph, R1, zp).wait_recv()
        part[s_next, :RANK, :] = part[s_next, :RANK, :] + rsr[ph * 6 + R1]
        ring_copy(part.at[s_next, low], ph, COMB_A, zp).start()
        ring_copy(part.at[s_prev, high], ph, R2, zm).wait_recv()
        part[s_prev, RANK:, :] = part[s_prev, RANK:, :] + rsr[ph * 6 + R2]
        ring_copy(part.at[s_prev, high], ph, COMB_B, zm).start()

    def finish(ph):
        s = slot_of(ph, 0)
        for slot in (RAW_A, RAW_B, COMB_A, COMB_B):
            ring_copy(part.at[s, low], ph, slot, zp).wait_recv()
        top = part[s, :RANK, :] + rsr[ph * 6 + RAW_A] + rsr[ph * 6 + COMB_A]
        bottom = part[s, RANK:, :] + rsr[ph * 6 + RAW_B] + rsr[ph * 6 + COMB_B]
        return gradient(top, bottom)

    w_copies[0].wait()
    project_out(range(2 * SPLIT))
    for copies in first[2:]:
        copies[0].start()
    for s in range(2 * SPLIT, AHEAD):
        start_item(s)
    pl.semaphore_wait(bar, NM - 1 + 6)
    for q in range(SPLIT):
        sib_half(q, low, q).start()
    for o in range(1, 4):
        pl.semaphore_signal(xsem, inc=1, device_id=(y * NX + (x + o) % NX, mp), device_id_type=MESH)
    w_copies[1].wait()
    for q in range(SPLIT):
        project_in((2 * q, 2 * q + 1))
        sib_half(q, high, PAIRS + q).start()
        for s in range(2 * q + AHEAD, 2 * q + 2 + AHEAD):
            start_item(s)
        if q == 0:
            for p in range(SPLIT):
                sib_half(p, low, p).wait_recv()
                part[2 * p + 1, :RANK, :] = part[2 * p + 1, :RANK, :] + sibr[p, :RANK, :]
                ring_copy(part.at[2 * p + 1, low], ORDER[p][0], R1, zp).start()

    def merge_high(p):
        sib_half(p, high, PAIRS + p).wait_recv()
        part[2 * p + 1, RANK:, :] = part[2 * p + 1, RANK:, :] + sibr[p, RANK:, :]
        ring_copy(part.at[2 * p + 1, high], ORDER[p][0], R2, zm).start()

    merge_high(0)

    def pair(q, carry):
        project_pair(q)
        sib_copy(q).start()
        start_item(2 * q + AHEAD)
        start_item(2 * q + 1 + AHEAD)
        @pl.when(q == SPLIT)
        def _():
            merge_high(1)

        @pl.when(q >= SPLIT + LAG)
        def _():
            merge(q - LAG)

        @pl.when(q == FORWARD_AT)
        def _():
            forward(0)

        return carry

    lax.fori_loop(SPLIT, PAIRS, pair, 0)
    for q in range(PAIRS - LAG, PAIRS):
        merge(q)
    forward(1)

    own_d, own_m = pl.ds(pl.multiple_of(dp * ROWS, ROWS), ROWS), pl.ds(pl.multiple_of(mp * ROWS, ROWS), ROWS)

    def mp_copy(o, src, dst, ss, rs):
        return pltpu.make_async_remote_copy(
            src_ref=src, dst_ref=dst.at[own_m], send_sem=ss, recv_sem=rs, device_id=(dp, (mp + o) % NM), device_id_type=MESH
        )

    def to_sibling(src, rows):
        return pltpu.make_async_remote_copy(
            src_ref=src, dst_ref=t_g.at[rows], send_sem=t_ss.at[1], recv_sem=t_rs.at[2],
            device_id=(dp, z * 2 + (1 - c)), device_id_type=MESH,
        )

    def dp_copy(o, src, dst, ss, rs):
        return pltpu.make_async_remote_copy(
            src_ref=src, dst_ref=dst.at[own_d], send_sem=ss, recv_sem=rs, device_id=((dp + o) % ND, mp), device_id_type=MESH
        )

    train_row = finish(0)
    t_own[...] = train_row
    pl.semaphore_wait(xsem, 3)
    for dz in range(1, NZ):
        mp_copy(2 * dz, t_own, t_g, t_ss.at[1], t_rs.at[1]).start()
    to_sibling(t_own, own_m).start()
    for o in range(1, ND):
        dp_copy(o, t_own, t_m, t_ss.at[0], t_rs.at[0]).start()
    t_m[own_d, :] = train_row
    t_g[own_m, :] = train_row

    target_row = finish(1)
    b_own[...] = target_row
    for o in range(1, NM):
        mp_copy(o, b_own, b_g, b_ss, b_rs).start()
    b_g[own_m, :] = target_row
    b_norm = jnp.sum(target_row * target_row)

    def bytes_of(ref, sem):
        return pltpu.make_async_copy(ref, ref, sem)

    dp_rest, mp_rest = pl.ds(0, (ND - 1) * ROWS), pl.ds(0, (NM - 1) * ROWS)
    bytes_of(t_g.at[pl.ds(0, (NZ - 1) * ROWS)], t_rs.at[1]).wait()
    for dz in range(1, NZ):
        rows = pl.ds(pl.multiple_of((((z + dz) % NZ) * 2 + c) * ROWS, ROWS), ROWS)
        to_sibling(t_g.at[rows], rows).start()
    bytes_of(t_m.at[dp_rest], t_rs.at[0]).wait()
    bytes_of(t_g.at[pl.ds(0, NZ * ROWS)], t_rs.at[2]).wait()
    place = ((mp + 1) % NM) * ND + dp
    msg[1:2, :] = jnp.where(iota((1, LANES), 1) == place, b_norm, block_row(t_g, t_m))
    bytes_of(b_g.at[mp_rest], b_rs).wait()
    msg[0:1, :] = block_row(b_g, t_m)

    me = dp * NM + mp

    to_dps = [((y + dy) % 4) * NX + (x + dx) % NX for dy in (2, 1, 3, 0) for dx in (2, 1, 3, 0)]
    to_mps = [((z + dz) % NZ) * 2 + (c + dc) % 2 for dz in (2, 1, 3, 0) for dc in (1, 0)]
    for to in [(to_dp, to_mp) for to_mp in to_mps for to_dp in to_dps][:-1]:
        pltpu.make_async_remote_copy(
            src_ref=msg, dst_ref=fin.at[me], send_sem=f_ss, recv_sem=f_rs, device_id=to, device_id_type=MESH
        ).start()
    fin[me] = msg[...]
    bytes_of(fin.at[pl.ds(0, NDEV - 1)], f_rs).wait()

    for d in range(ND):
        rows, spaced = pl.ds(d * NM, NM), pl.ds(d, NM, stride=ND)
        c_mat[spaced, :] = swap_blocks(fin[rows, 0, :])
        k_mat[spaced, :] = swap_blocks(fin[rows, 1, :])
    lane, sub = iota((NDEV, LANES), 1), iota((NDEV, LANES), 0)
    sent = k_mat[...]
    taken = sub == (lane + ND) % LANES
    norm = jnp.sum(jnp.where(taken, sent, 0.0), axis=0, keepdims=True)
    mirror = jnp.sum(jnp.where(lane == sub, pltpu.roll(sent, LANES - ND, 1), 0.0), axis=0, keepdims=True)
    gram = jnp.where(taken, mirror, sent)
    trace = jnp.sum(jnp.where(lane == sub, gram, 0.0), axis=0, keepdims=True)
    damping = jnp.sum(trace, axis=1, keepdims=True) * (0.1 / (NDEV * RANK * RANK))
    inv = 1.0 / NDEV
    g_first, g_second, g_third = thirds(gram)
    gram_leading = jnp.concatenate(
        [jnp.concatenate([g_first, g_first], axis=1), jnp.concatenate([g_second, g_second], axis=1)], axis=0
    )
    gram_rest = jnp.concatenate([g_third, g_first], axis=1)
    u_res = c_mat[...].T
    u_dir, scores, dir_norm = u_res, jnp.zeros_like(u_res), norm
    for step in range(ITERS):
        u_norm = jnp.sum(u_dir * u_dir, axis=0, keepdims=True)
        alpha = norm / (damping * dir_norm + u_norm * inv)
        scores = scores + alpha * u_dir
        if step == ITERS - 1:
            break
        u_first, u_second, u_third = thirds(u_dir)
        leading = jnp.dot(gram_leading, jnp.concatenate([u_first, u_second], axis=0), preferred_element_type=F32)
        rest = jnp.dot(gram_rest, jnp.concatenate([u_first, u_third], axis=0), preferred_element_type=F32)
        image = (rest + leading[NDEV:, :]) + leading[:NDEV, :]
        u_gram = jnp.sum(u_dir * image, axis=0, keepdims=True)
        squared = damping * damping * dir_norm + 2.0 * inv * damping * u_norm + inv * inv * u_gram
        following = alpha * alpha * squared - norm
        u_res = u_res - alpha * (damping * u_dir + inv * image)
        ratio = following / norm
        u_dir = u_res + ratio * u_dir
        dir_norm = following + ratio * ratio * dir_norm
        norm = following
    row = jnp.sum(jnp.where(sub == mp * ND + dp, scores, 0.0), axis=0, keepdims=True)
    column = jnp.sum(jnp.where(lane == sub, row, 0.0), axis=1, keepdims=True)
    spread = jnp.where(lane == (sub % ND) * NM + sub // ND, column, 0.0)
    out_ref[...] = sum(spread[8 * d : 8 * d + 8, :] for d in range(ND))

    bytes_of(part.at[pl.ds(0, PAIRS)], sib_ss).wait()
    bytes_of(rsr, rs_ss).wait()
    bytes_of(t_m.at[dp_rest], t_ss.at[0]).wait()
    bytes_of(t_g.at[mp_rest], t_ss.at[1]).wait()
    bytes_of(b_g.at[mp_rest], b_ss).wait()
    bytes_of(fin.at[pl.ds(0, NDEV - 1)], f_ss).wait()


def local(train_in, train_grad_out, target_in, target_grad_out, proj_in, proj_out):
    d_in, d_out = proj_in.shape[1], proj_out.shape[1]
    dma, vmem = pltpu.SemaphoreType.DMA, pltpu.VMEM
    spread = pl.pallas_call(
        kernel,
        out_shape=jax.ShapeDtypeStruct((8, NDEV), F32),
        in_specs=[pl.BlockSpec(memory_space=pltpu.HBM)] * 6,
        out_specs=pl.BlockSpec(memory_space=pltpu.VMEM),
        scratch_shapes=[
            vmem((2 * PAIRS, d_in, SEQ), BF16),
            vmem((2 * PAIRS, SEQ, d_out), BF16),
            vmem((RANK, d_in), BF16),
            vmem((RANK, d_out), BF16),
            vmem((2 * PAIRS, 2 * RANK, SEQ), F32),
            vmem((PAIRS, 2 * RANK, SEQ), F32),
            vmem((12, RANK, SEQ), F32),
            vmem((ROWS, LANES), F32),
            vmem((ROWS, LANES), F32),
            vmem((ND * ROWS, LANES), F32),
            vmem((NM * ROWS, LANES), F32),
            vmem((NM * ROWS, LANES), F32),
            vmem((2, LANES), F32),
            vmem((NDEV, 2, LANES), F32),
            vmem((NDEV, LANES), F32),
            vmem((NDEV, LANES), F32),
            dma((2 * PAIRS, 2)),
            dma((2,)),
            dma,
            dma((PAIRS + SPLIT,)),
            dma,
            dma((12,)),
            dma((2,)),
            dma((3,)),
            dma,
            dma,
            dma,
            dma,
            pltpu.SemaphoreType.REGULAR,
        ],
        compiler_params=pltpu.CompilerParams(collective_id=0, has_side_effects=True, vmem_limit_bytes=32 * 1024 * 1024),
    )(*(
        pltpu.with_memory_space_constraint(a, pltpu.HBM)
        for a in (train_in.swapaxes(1, 2), train_grad_out, target_in.swapaxes(1, 2), target_grad_out, proj_in, proj_out)
    ))
    return jnp.sum(spread, axis=0, keepdims=True)


def solution(mesh):
    return jax.shard_map(
        local,
        mesh=mesh,
        in_specs=(
            P("dp", None, "mp"),
            P("dp", None, "mp"),
            P("dp", None, "mp"),
            P("dp", None, "mp"),
            P(None, "mp"),
            P(None, "mp"),
        ),
        out_specs=P(("dp", "mp"), None),
        check_vma=False,
    )
```
